32 devices in a mesh: days: 2 (over y), chan: 8 (over z, x), win: 2 (over core).
Axes of the slice: x: 2, y: 2, z: 4, core: 2. Of those that a mesh axis runs over, the one named last changes fastest.
Arguments:
- records: bfloat16 [2048, 2, 3000], P(('days', 'chan'), 'win'), parts along dimension 0, may hold values from -6 to 6
- assign: int32 [1024], P('chan'), may hold values from 0 to 127, as said below
- plan: int32 [1], replicated, may hold values from 0 to 2
- seg_mask: int32 [16, 2], P(('days', 'chan'), 'win'), parts along dimension 0, may hold values 0 or 1
Outputs:
- correlations: float32 [2, 1024, 128, 64], P('days', 'chan', 'win'), parts along dimension 0
The draws below stay inside these ranges and needn't reach their ends.
There are 2 independent parts, one for each index of `days`. The reference program is written for one: setup_inputs(seed, part) draws one part's arguments, and reference() takes and returns one part's arrays. A program takes and returns all parts, laid end to end along the dimension named above; an argument that names none is the same for every part. Nothing has to cross between parts.
Inputs may be any that keep to these rules, and one draw needn't show every extreme that they name: `assign`: each aligned group of 128 entries holds every number from 0 to 127 once.
All inputs are finite; a program needn't handle non-finite values. No bound on the sum of `seg_mask` on one device may be relied on, other than what follows from the above.
Results may differ from the reference program's by a relative error of at most 0.005.
Values may be sent and summed in bfloat16 or wider, within the bound.
A program may use at most 64 MiB of HBM per device.

```python
import jax
import jax.numpy as jnp
from jax import lax

BLOCK_CH = 128
SEG_LEN = 3000
LAGS = 64
SEG_DEV = 1
ROUNDS = 1
BLOCKS = 8
CHANNELS = 1024
SEGMENTS = 2
CHAN_BITS = 3
N_WIN = 2


def draw_assign(key, part):
    sub_keys = jax.random.split(jax.random.fold_in(key, 17), BLOCKS)
    shuffles = jax.vmap(lambda one_key: jax.random.permutation(one_key, BLOCK_CH))(sub_keys)
    return shuffles.reshape(-1).astype(jnp.int32)


def set_ends(array, stream_key, least, top_value):
    index_at = [jax.random.randint(jax.random.fold_in(stream_key, axis), (), 0, length) for axis, length in enumerate(array.shape)]
    longest = array.shape.index(max(array.shape))
    neighbour = index_at[:longest] + [(index_at[longest] + 1) % array.shape[longest]] + index_at[longest + 1:]
    return array.at[tuple(index_at)].set(least).at[tuple(neighbour)].set(top_value)


def levels(key, shape, cuts, smallest, high):
    def one(dim, blocks):
        steps = jax.random.uniform(jax.random.fold_in(jax.random.fold_in(key, 6), dim), (blocks,), jnp.float32, smallest / len(cuts), high / len(cuts))
        return jnp.repeat(jnp.exp(steps), shape[dim] // blocks).reshape((-1,) + (1,) * (len(shape) - dim - 1))

    loudness = one(*cuts[0])
    for cut in cuts[1:]:
        loudness = loudness * one(*cut)
    return loudness


def normal_values(rng, shape, deviation, reach, pieces=(), kind=jnp.bfloat16):
    entries = deviation * jax.random.normal(rng, shape, jnp.float32)
    if pieces:
        entries = entries * levels(rng, shape, pieces, -0.22, 0.18)
    return jnp.clip(entries, -reach, reach).astype(kind)


def setup_inputs(seed: int = 0, part: int = 0) -> dict:
    key_list = jax.random.split(jax.random.key(seed), 5)
    part_keys = jax.random.split(jax.random.fold_in(key_list[4], part), 5)
    records = normal_values(part_keys[0], (CHANNELS, SEGMENTS, SEG_LEN), 1.0, 6.0, ((0, 8), (1, 2)))
    assign = draw_assign(jax.random.fold_in(key_list[4], 71), part)
    plan = jax.random.randint(key_list[2], (ROUNDS,), 0, CHAN_BITS).astype(jnp.int32)
    seg_mask = set_ends((jax.random.randint(part_keys[3], (BLOCKS, SEGMENTS), 0, 4) < 3).astype(jnp.int32), jax.random.fold_in(part_keys[3], 1), 0, 1)
    return dict(records=records, assign=assign, plan=plan, seg_mask=seg_mask)


def correlate_pair(own_block, partner_block, mask_own, mask_partner):
    own_f = own_block.astype(jnp.float32) * mask_own[None, :, None]
    partner_f = partner_block.astype(jnp.float32) * mask_partner[None, :, None]
    lag_half = LAGS // 2
    padded = jnp.pad(partner_f, ((0, 0), (0, 0), (lag_half, lag_half)))
    own_split = own_f.reshape(BLOCK_CH, N_WIN, SEG_DEV, SEG_LEN)

    def lag_term(lag_pos):
        shifted = lax.dynamic_slice_in_dim(padded, lag_pos, SEG_LEN, 2)
        shifted = shifted.reshape(BLOCK_CH, N_WIN, SEG_DEV, SEG_LEN)
        return jnp.einsum('iwst,jwst->wij', own_split, shifted)
    lag_terms = lax.map(lag_term, jnp.arange(LAGS, dtype=jnp.int32))
    rounded = lax.optimization_barrier(lag_terms.astype(jnp.bfloat16)).astype(jnp.float32)
    stacked = lax.optimization_barrier(jnp.sum(rounded, axis=1))
    valid_count = jnp.sum(mask_own * mask_partner)
    normed = stacked / (jnp.maximum(valid_count, 1.0) * jnp.sqrt(jnp.float32(SEG_LEN)))
    return jnp.transpose(normed, (1, 2, 0))

def reference(records, assign, plan, seg_mask):
    blocked = records.reshape(BLOCKS, BLOCK_CH, SEGMENTS, SEG_LEN)
    slots = assign.reshape(BLOCKS, BLOCK_CH).astype(jnp.int32)
    ordered = jnp.take_along_axis(blocked, slots[:, :, None, None], axis=1)
    masks = seg_mask.astype(jnp.float32)
    block_ids = jnp.arange(BLOCKS, dtype=jnp.int32)
    results = []
    for round_num in range(ROUNDS):
        flip = jnp.left_shift(jnp.int32(1), plan[round_num].astype(jnp.int32)).astype(jnp.int32)
        partners = jnp.bitwise_xor(block_ids, flip).astype(jnp.int32)

        def one_block(block_num):
            partner = partners[block_num]
            return correlate_pair(ordered[block_num], ordered[partner], masks[block_num], masks[partner])
        per_block = lax.map(one_block, block_ids)
        results.append(per_block.reshape(CHANNELS, BLOCK_CH, LAGS))
    return jnp.stack(results, 0)
```

```python
import functools
import math

import jax
import jax.numpy as jnp
from jax import lax
from jax.experimental import pallas as pl
from jax.experimental.pallas import tpu as pltpu
from jax.sharding import PartitionSpec as P

LAGS = 64
HALF = LAGS // 2
STEP = 16
GROUPS = LAGS // STEP
CHUNK = 512
FRONT = LAGS
MESH = pl.DeviceIdType.MESH


def kernel(
    bit,
    rec_ref,
    assign_ref,
    mask_ref,
    out_ref,
    valid_ref,
    base,
    shifted,
    part_send,
    part_recv,
    total,
    term_send,
    term_recv,
    cnt_send,
    cnt_recv,
    psend_sem,
    precv_sem,
    tsend_sem,
    trecv_sem,
    csem,
):
    span, rows = rec_ref.shape
    chunks = span // CHUNK
    own = lax.axis_index("chan")
    win = lax.axis_index("win")
    digit = 1 << bit
    partner = own + digit - 2 * digit * (own // digit % 2)
    sibling = 1 - win
    keep = rows // 2

    barrier = pltpu.get_barrier_semaphore()
    pl.semaphore_signal(barrier, inc=1, device_id={"chan": partner}, device_id_type=MESH)
    pl.semaphore_signal(barrier, inc=1, device_id={"win": sibling}, device_id_type=MESH)

    mask = mask_ref[...].astype(jnp.float32)
    hit = lax.broadcasted_iota(jnp.int32, (rows, rows), 0) == assign_ref[...]
    table_t = jnp.where(hit, jnp.broadcast_to(mask, (rows, rows)), 0.0)
    table = table_t.T.astype(jnp.bfloat16)
    table_t = table_t.astype(jnp.bfloat16)
    pl.semaphore_wait(barrier, 2)

    def part_copy(c):
        return pltpu.make_async_remote_copy(
            src_ref=part_send.at[c],
            dst_ref=part_recv.at[c],
            send_sem=psend_sem.at[c],
            recv_sem=precv_sem.at[c],
            device_id={"chan": partner},
            device_id_type=MESH,
        )

    def send_part(c, _):
        block = rec_ref[pl.ds(pl.multiple_of(c * CHUNK, CHUNK), CHUNK), :]
        ordered = lax.dot_general(
            table, block, (((1,), (1,)), ((), ())), preferred_element_type=jnp.float32
        )
        col = lax.broadcasted_iota(jnp.int32, (rows, CHUNK), 1)
        ordered = jnp.where(
            (col == CHUNK - 1) & (c == chunks - 1), jnp.broadcast_to(mask, ordered.shape), ordered
        )
        part_send[c] = ordered.astype(jnp.bfloat16)
        part_copy(c).start()
        return 0

    lax.fori_loop(0, chunks, send_part, 0)

    base[pl.ds(0, FRONT), :] = jnp.zeros((FRONT, rows), jnp.float32)
    tail = base.shape[0] - FRONT - span
    base[pl.ds(FRONT + span, tail), :] = jnp.zeros((tail, rows), jnp.float32)

    def fill(c, _):
        at = pl.multiple_of(c * CHUNK, CHUNK)
        base[pl.ds(FRONT + at, CHUNK), :] = jnp.dot(
            rec_ref[pl.ds(at, CHUNK), :], table_t, preferred_element_type=jnp.float32
        )
        return 0

    lax.fori_loop(0, chunks, fill, 0)

    height = 80

    def spread(b, _):
        at = pl.multiple_of(b * height, 16)
        for s in range(STEP):
            shifted[pl.ds(at, height), s * rows : (s + 1) * rows] = base[
                pl.ds(at + FRONT - STEP - s, height), :
            ].astype(jnp.bfloat16)
        return 0

    lax.fori_loop(0, shifted.shape[0] // height, spread, 0)

    def products(c, a):
        at = pl.multiple_of(c * CHUNK + (GROUPS - 1 - a) * STEP, STEP)
        return jnp.dot(
            part_recv[c], shifted[pl.ds(at, CHUNK), :], preferred_element_type=jnp.float32
        )

    part_copy(0).wait_recv()
    for a in range(GROUPS):
        total[a] = products(0, a)

    def middle(c, _):
        part_copy(c).wait_recv()
        for a in range(GROUPS):
            total[a] += products(c, a)
        return 0

    lax.fori_loop(1, chunks - 1, middle, 0)

    last = chunks - 1
    part_copy(last).wait_recv()
    both = part_recv[last, 0:16, CHUNK - 128 :].astype(jnp.float32)[0:8, 127:128] * mask
    both = jnp.broadcast_to(both, (8, 128))
    cnt_send[...] = jnp.broadcast_to(both[0:1, :], (16, 128)).astype(jnp.bfloat16)
    cnt_copy = pltpu.make_async_remote_copy(
        src_ref=cnt_send,
        dst_ref=cnt_recv,
        send_sem=csem.at[0],
        recv_sem=csem.at[1],
        device_id={"win": sibling},
        device_id_type=MESH,
    )
    cnt_copy.start()

    def term_copy(a):
        return pltpu.make_async_remote_copy(
            src_ref=term_send.at[a],
            dst_ref=term_recv.at[a],
            send_sem=tsend_sem.at[a],
            recv_sem=trecv_sem.at[a],
            device_id={"win": sibling},
            device_id_type=MESH,
        )

    theirs = pl.ds(pl.multiple_of(sibling * keep, keep), keep)
    mine = pl.ds(pl.multiple_of(win * keep, keep), keep)
    for a in range(GROUPS):
        total[a] += products(last, a)
        term_send[a] = total[a, theirs, :].astype(jnp.bfloat16)
        term_copy(a).start()

    for a in range(GROUPS):
        term_copy(a).wait_recv()
        for s in range(STEP):
            lanes = slice(s * rows, (s + 1) * rows)
            kept = total[a, mine, lanes].astype(jnp.bfloat16).astype(jnp.float32)
            out_ref[:, a * STEP + s, :] = kept + term_recv[a, :, lanes].astype(jnp.float32)

    cnt_copy.wait_recv()
    valid_ref[...] = both + cnt_recv[...].astype(jnp.float32)[0:8, :]

    cnt_copy.wait_send()
    for a in range(GROUPS):
        term_copy(a).wait_send()

    def drain(c, _):
        part_copy(c).wait_send()
        return 0

    lax.fori_loop(0, chunks, drain, 0)


def correlate(bit, rec, assign, mask):
    span, rows = rec.shape
    chunks = span // CHUNK
    keep = rows // 2
    wide = STEP * rows
    tall = span + (GROUPS - 1) * STEP
    tall += -tall % 80
    vmem = pl.BlockSpec(memory_space=pltpu.VMEM)
    return pl.pallas_call(
        functools.partial(kernel, bit),
        out_shape=(
            jax.ShapeDtypeStruct((keep, LAGS, rows), jnp.float32),
            jax.ShapeDtypeStruct((8, 128), jnp.float32),
        ),
        in_specs=[vmem] * 3,
        out_specs=(vmem, vmem),
        scratch_shapes=[
            pltpu.VMEM((tall + FRONT - STEP + 16, rows), jnp.float32),
            pltpu.VMEM((tall, wide), jnp.bfloat16),
            pltpu.VMEM((chunks, rows, CHUNK), jnp.bfloat16),
            pltpu.VMEM((chunks, rows, CHUNK), jnp.bfloat16),
            pltpu.VMEM((GROUPS, rows, wide), jnp.float32),
            pltpu.VMEM((GROUPS, keep, wide), jnp.bfloat16),
            pltpu.VMEM((GROUPS, keep, wide), jnp.bfloat16),
            pltpu.VMEM((16, 128), jnp.bfloat16),
            pltpu.VMEM((16, 128), jnp.bfloat16),
            pltpu.SemaphoreType.DMA((chunks,)),
            pltpu.SemaphoreType.DMA((chunks,)),
            pltpu.SemaphoreType.DMA((GROUPS,)),
            pltpu.SemaphoreType.DMA((GROUPS,)),
            pltpu.SemaphoreType.DMA((2,)),
        ],
        compiler_params=pltpu.CompilerParams(
            collective_id=bit, has_side_effects=True, vmem_limit_bytes=48 * 1024 * 1024
        ),
    )(rec, assign, mask)


def body(records, assign, plan, seg_mask):
    rows, segs, seg_len = records.shape
    assert segs == 1 and lax.axis_size("win") == 2
    span = seg_len + LAGS
    span += -span % CHUNK
    rec = jnp.pad(records.reshape(rows, seg_len).T, ((0, span - seg_len), (0, 0)))
    digits = lax.axis_size("chan").bit_length() - 1
    branches = [functools.partial(correlate, bit) for bit in range(digits)]
    stacked, valid = lax.switch(
        plan[0], branches, rec, assign.reshape(1, rows), seg_mask.reshape(1, 1)
    )
    normed = stacked / (jnp.maximum(valid[0, 0], 1.0) * math.sqrt(seg_len))
    return jnp.transpose(normed, (2, 0, 1))[None]


def solution(mesh):
    placed = (P(("days", "chan"), "win", None), P("chan"), P(), P(("days", "chan"), "win"))
    return jax.shard_map(
        body, mesh=mesh, in_specs=placed, out_specs=P("days", "chan", "win", None), check_vma=False
    )
```

```python
import functools
import math

import jax
import jax.numpy as jnp
from jax import lax
from jax.experimental import pallas as pl
from jax.experimental.pallas import tpu as pltpu
from jax.sharding import PartitionSpec as P

LAGS = 64
HALF = LAGS // 2
STEP = 8
GROUPS = LAGS // STEP
CHUNK = 512
FRONT = LAGS
LANES = 128
MARK = 16
MESH = pl.DeviceIdType.MESH


def kernel(
    bit,
    rec_ref,
    assign_ref,
    mask_ref,
    out_ref,
    base,
    shifted,
    part_send,
    part_recv,
    own_send,
    own_recv,
    lhs,
    total,
    psend_sem,
    precv_sem,
    osend_sem,
    orecv_sem,
):
    seg_len, rows = rec_ref.shape
    span = shifted.shape[1]
    chunks = span // CHUNK
    last = chunks - 1
    left = seg_len - last * CHUNK
    own = lax.axis_index("chan")
    win = lax.axis_index("win")
    digit = 1 << bit
    partner = own + digit - 2 * digit * (own // digit % 2)
    sibling = 1 - win
    keep = rows // 2

    barrier = pltpu.get_barrier_semaphore()
    for there in ({"chan": partner}, {"chan": partner, "win": sibling}, {"win": sibling}):
        pl.semaphore_signal(barrier, inc=1, device_id=there, device_id_type=MESH)

    mask = mask_ref[...].astype(jnp.float32)
    hit = lax.broadcasted_iota(jnp.int32, (rows, rows), 0) == assign_ref[...]
    table_t = jnp.where(hit, jnp.broadcast_to(mask, (rows, rows)), 0.0)
    table = table_t.T.astype(jnp.bfloat16)
    table_t = table_t.astype(jnp.bfloat16)

    def part_copies(c):
        halves = []
        for place, (side, there) in enumerate(
            ((win, {"chan": partner}), (sibling, {"chan": partner, "win": sibling}))
        ):
            halves.append(
                pltpu.make_async_remote_copy(
                    src_ref=part_send.at[c, pl.ds(pl.multiple_of(side * keep, keep), keep)],
                    dst_ref=part_recv.at[place, c],
                    send_sem=psend_sem.at[place, c],
                    recv_sem=precv_sem.at[place, c],
                    device_id=there,
                    device_id_type=MESH,
                )
            )
        return halves

    def own_copy(c):
        return pltpu.make_async_remote_copy(
            src_ref=own_send.at[c],
            dst_ref=own_recv.at[c],
            send_sem=osend_sem.at[c],
            recv_sem=orecv_sem.at[c],
            device_id={"win": sibling},
            device_id_type=MESH,
        )

    def block_of(c):
        return rec_ref[pl.ds(pl.multiple_of(c * CHUNK, CHUNK), CHUNK), :]

    tail = jnp.concatenate(
        [
            rec_ref[pl.ds(last * CHUNK, left), :].astype(jnp.float32),
            jnp.zeros((CHUNK - left, rows), jnp.float32),
        ],
        axis=0,
    ).astype(jnp.bfloat16)

    def arrange(block):
        return lax.dot_general(
            table, block, (((1,), (1,)), ((), ())), preferred_element_type=jnp.float32
        )

    def send_part(c, _):
        part_send[c] = arrange(block_of(c)).astype(jnp.bfloat16)

        @pl.when(c == 0)
        def _():
            pl.semaphore_wait(barrier, 3)

        for copy in part_copies(c):
            copy.start()
        return 0

    lax.fori_loop(0, last, send_part, 0)
    col = lax.broadcasted_iota(jnp.int32, (rows, CHUNK), 1)
    ordered = arrange(tail)
    ordered = jnp.where(col == CHUNK - 1, jnp.broadcast_to(mask, ordered.shape), ordered)
    part_send[last] = ordered.astype(jnp.bfloat16)
    for copy in part_copies(last):
        copy.start()

    base[pl.ds(0, FRONT), :] = jnp.zeros((FRONT, rows), jnp.float32)

    def fill(c, _):
        at = pl.multiple_of(c * CHUNK, CHUNK)
        turned = jnp.dot(block_of(c), table_t, preferred_element_type=jnp.float32)
        base[pl.ds(FRONT + at, CHUNK), :] = turned
        own_send[c] = turned.astype(jnp.bfloat16)
        own_copy(c).start()
        return 0

    lax.fori_loop(0, last, fill, 0)
    row = lax.broadcasted_iota(jnp.int32, (CHUNK, rows), 0)
    turned = jnp.dot(tail, table_t, preferred_element_type=jnp.float32)
    base[pl.ds(FRONT + last * CHUNK, CHUNK), :] = turned
    turned = jnp.where(row >= CHUNK - MARK, jnp.broadcast_to(mask, turned.shape), turned)
    own_send[last] = turned.astype(jnp.bfloat16)
    own_copy(last).start()

    height = 64

    def spread(place):
        def one(b, _):
            at = pl.multiple_of(b * height, height)
            for s in range(STEP):
                shifted[place, pl.ds(at, height), s * rows : (s + 1) * rows] = base[
                    pl.ds(at + FRONT - HALF + STEP - s, height), :
                ].astype(jnp.bfloat16)
            return 0

        lax.fori_loop(0, span // height, one, 0)

    spread(0)

    def refill(c, _):
        at = pl.multiple_of(c * CHUNK, CHUNK)
        own_copy(c).wait_recv()
        base[pl.ds(FRONT + at, CHUNK), :] = own_recv[c].astype(jnp.float32)
        return 0

    lax.fori_loop(0, last, refill, 0)
    own_copy(last).wait_recv()
    arrived = own_recv[last].astype(jnp.float32)
    mask_sibling = arrived[CHUNK - 8 :, :]
    base[pl.ds(FRONT + last * CHUNK, CHUNK), :] = jnp.where(row >= CHUNK - MARK, 0.0, arrived)
    spread(1)

    def load(place, c, before):
        block = part_recv[place, c].astype(jnp.float32)
        if before is None:
            edge = jnp.zeros((keep, LANES), jnp.float32)
        else:
            edge = part_recv[place, before, :, CHUNK - LANES :].astype(jnp.float32)
        joined = jnp.concatenate([edge, block], axis=1)
        for a in range(GROUPS):
            start = LANES - (GROUPS - 1 - a) * STEP
            lhs[place, a * keep : (a + 1) * keep, :] = joined[:, start : start + CHUNK].astype(
                jnp.bfloat16
            )

    def product(place, c, lanes):
        at = pl.multiple_of(c * CHUNK, CHUNK)
        return jnp.dot(
            lhs[place], shifted[place, pl.ds(at, CHUNK), lanes], preferred_element_type=jnp.float32
        )

    quarters = [slice(q * 2 * rows, (q + 1) * 2 * rows) for q in range(STEP // 2)]

    def arrive(c, before):
        for place, copy in enumerate(part_copies(c)):
            copy.wait_recv()
            load(place, c, before)

    arrive(0, None)
    for lanes in quarters:
        total[:, lanes] = product(0, 0, lanes) + product(1, 0, lanes)

    def middle(c, _):
        arrive(c, c - 1)
        for lanes in quarters:
            total[:, lanes] += product(0, c, lanes) + product(1, c, lanes)
        return 0

    lax.fori_loop(1, last, middle, 0)

    arrive(last, last - 1)
    marks = [
        part_recv[place, last, 0:MARK, CHUNK - LANES :].astype(jnp.float32)[
            0:8, LANES - 1 : LANES
        ]
        for place in range(2)
    ]
    valid = marks[0] * mask + marks[1] * mask_sibling
    scale = (1.0 / (jnp.maximum(valid, 1.0) * math.sqrt(seg_len)))[0:1, :]
    for q, lanes in enumerate(quarters):
        done = total[:, lanes] + product(0, last, lanes) + product(1, last, lanes)
        for s in range(2):
            for a in range(GROUPS):
                out_ref[:, a * STEP + 2 * q + s, :] = (
                    done[a * keep : (a + 1) * keep, s * rows : (s + 1) * rows] * scale
                )

    def drain(c, _):
        for copy in part_copies(c):
            copy.wait_send()
        own_copy(c).wait_send()
        return 0

    lax.fori_loop(0, chunks, drain, 0)


def correlate(bit, rec, assign, mask):
    seg_len, rows = rec.shape
    span = seg_len + LAGS
    span += -span % CHUNK
    chunks = span // CHUNK
    keep = rows // 2
    vmem = pl.BlockSpec(memory_space=pltpu.VMEM)
    return pl.pallas_call(
        functools.partial(kernel, bit),
        out_shape=jax.ShapeDtypeStruct((keep, LAGS, rows), jnp.float32),
        in_specs=[vmem] * 3,
        out_specs=vmem,
        scratch_shapes=[
            pltpu.VMEM((span + FRONT, rows), jnp.float32),
            pltpu.VMEM((2, span, STEP * rows), jnp.bfloat16),
            pltpu.VMEM((chunks, rows, CHUNK), jnp.bfloat16),
            pltpu.VMEM((2, chunks, keep, CHUNK), jnp.bfloat16),
            pltpu.VMEM((chunks, CHUNK, rows), jnp.bfloat16),
            pltpu.VMEM((chunks, CHUNK, rows), jnp.bfloat16),
            pltpu.VMEM((2, GROUPS * keep, CHUNK), jnp.bfloat16),
            pltpu.VMEM((GROUPS * keep, STEP * rows), jnp.float32),
            pltpu.SemaphoreType.DMA((2, chunks)),
            pltpu.SemaphoreType.DMA((2, chunks)),
            pltpu.SemaphoreType.DMA((chunks,)),
            pltpu.SemaphoreType.DMA((chunks,)),
        ],
        compiler_params=pltpu.CompilerParams(
            collective_id=bit, has_side_effects=True, vmem_limit_bytes=48 * 1024 * 1024
        ),
    )(rec, assign, mask)


def body(records, assign, plan, seg_mask):
    rows, segs, seg_len = records.shape
    assert segs == 1 and lax.axis_size("win") == 2
    rec = records.reshape(rows, seg_len).T
    digits = lax.axis_size("chan").bit_length() - 1
    branches = [functools.partial(correlate, bit) for bit in range(digits)]
    normed = lax.switch(plan[0], branches, rec, assign.reshape(1, rows), seg_mask.reshape(1, 1))
    return jnp.transpose(normed, (2, 0, 1))[None]


def solution(mesh):
    placed = (P(("days", "chan"), "win", None), P("chan"), P(), P(("days", "chan"), "win"))
    return jax.shard_map(
        body, mesh=mesh, in_specs=placed, out_specs=P("days", "chan", "win", None), check_vma=False
    )
```

```python
import functools
import math

import jax
import jax.numpy as jnp
from jax import lax
from jax.experimental import pallas as pl
from jax.experimental.pallas import tpu as pltpu
from jax.sharding import PartitionSpec as P

LAGS = 64
HALF = LAGS // 2
STEP = 8
GROUPS = LAGS // STEP
CHUNK = 256
FRONT = LAGS
LANES = 128
MARK = 16
MESH = pl.DeviceIdType.MESH


def kernel(
    bit,
    rec_hbm,
    assign_hbm,
    mask_hbm,
    out_ref,
    rec_ref,
    assign_ref,
    mask_ref,
    base,
    shifted,
    part_send,
    part_recv,
    own_send,
    own_recv,
    lhs,
    total,
    psend_sem,
    precv_sem,
    osend_sem,
    orecv_sem,
    load_sem,
):
    seg_len, rows = rec_ref.shape
    span = shifted.shape[1]
    chunks = span // CHUNK
    last = chunks - 1
    left = seg_len - last * CHUNK
    own = lax.axis_index("chan")
    win = lax.axis_index("win")
    digit = 1 << bit
    partner = own + digit - 2 * digit * (own // digit % 2)
    sibling = 1 - win
    keep = rows // 2

    barrier = pltpu.get_barrier_semaphore()
    for there in ({"chan": partner}, {"chan": partner, "win": sibling}, {"win": sibling}):
        pl.semaphore_signal(barrier, inc=1, device_id=there, device_id_type=MESH)
    loads = [
        pltpu.make_async_copy(src, dst, load_sem.at[n])
        for n, (src, dst) in enumerate(
            ((assign_hbm, assign_ref), (mask_hbm, mask_ref), (rec_hbm, rec_ref))
        )
    ]
    for copy in loads:
        copy.start()
    loads[0].wait()
    loads[1].wait()

    mask = mask_ref[...].astype(jnp.float32)
    hit = lax.broadcasted_iota(jnp.int32, (rows, rows), 0) == assign_ref[...]
    table_t = jnp.where(hit, jnp.broadcast_to(mask, (rows, rows)), 0.0)
    table = table_t.T.astype(jnp.bfloat16)
    table_t = table_t.astype(jnp.bfloat16)

    def part_copies(c):
        halves = []
        for place, (side, there) in enumerate(
            ((win, {"chan": partner}), (sibling, {"chan": partner, "win": sibling}))
        ):
            halves.append(
                pltpu.make_async_remote_copy(
                    src_ref=part_send.at[c, pl.ds(pl.multiple_of(side * keep, keep), keep)],
                    dst_ref=part_recv.at[place, c],
                    send_sem=psend_sem.at[place, c],
                    recv_sem=precv_sem.at[place, c],
                    device_id=there,
                    device_id_type=MESH,
                )
            )
        return halves

    def own_copy(c):
        return pltpu.make_async_remote_copy(
            src_ref=own_send.at[c],
            dst_ref=own_recv.at[c],
            send_sem=osend_sem.at[c],
            recv_sem=orecv_sem.at[c],
            device_id={"win": sibling},
            device_id_type=MESH,
        )

    def block_of(c):
        return rec_ref[pl.ds(pl.multiple_of(c * CHUNK, CHUNK), CHUNK), :]

    loads[2].wait()
    tail = jnp.concatenate(
        [
            rec_ref[pl.ds(last * CHUNK, left), :].astype(jnp.float32),
            jnp.zeros((CHUNK - left, rows), jnp.float32),
        ],
        axis=0,
    ).astype(jnp.bfloat16)

    def arrange(block):
        return lax.dot_general(
            table, block, (((1,), (1,)), ((), ())), preferred_element_type=jnp.float32
        )

    def send_part(c, _):
        part_send[c] = arrange(block_of(c)).astype(jnp.bfloat16)

        @pl.when(c == 0)
        def _():
            pl.semaphore_wait(barrier, 3)

        for copy in part_copies(c):
            copy.start()
        return 0

    lax.fori_loop(0, last, send_part, 0)
    col = lax.broadcasted_iota(jnp.int32, (rows, CHUNK), 1)
    ordered = arrange(tail)
    ordered = jnp.where(col == CHUNK - 1, jnp.broadcast_to(mask, ordered.shape), ordered)
    part_send[last] = ordered.astype(jnp.bfloat16)
    for copy in part_copies(last):
        copy.start()

    base[pl.ds(0, FRONT), :] = jnp.zeros((FRONT, rows), jnp.float32)

    def fill(c, _):
        at = pl.multiple_of(c * CHUNK, CHUNK)
        turned = jnp.dot(block_of(c), table_t, preferred_element_type=jnp.float32)
        base[pl.ds(FRONT + at, CHUNK), :] = turned
        own_send[c] = turned.astype(jnp.bfloat16)
        own_copy(c).start()
        return 0

    lax.fori_loop(0, last, fill, 0)
    row = lax.broadcasted_iota(jnp.int32, (CHUNK, rows), 0)
    turned = jnp.dot(tail, table_t, preferred_element_type=jnp.float32)
    base[pl.ds(FRONT + last * CHUNK, CHUNK), :] = turned
    turned = jnp.where(row >= CHUNK - MARK, jnp.broadcast_to(mask, turned.shape), turned)
    own_send[last] = turned.astype(jnp.bfloat16)
    own_copy(last).start()

    height = 64

    def spread(place):
        def one(b, _):
            at = pl.multiple_of(b * height, height)
            for s in range(STEP):
                shifted[place, pl.ds(at, height), s * rows : (s + 1) * rows] = base[
                    pl.ds(at + FRONT - HALF + STEP - s, height), :
                ].astype(jnp.bfloat16)
            return 0

        lax.fori_loop(0, span // height, one, 0)

    spread(0)

    def refill(c, _):
        at = pl.multiple_of(c * CHUNK, CHUNK)
        own_copy(c).wait_recv()
        base[pl.ds(FRONT + at, CHUNK), :] = own_recv[c].astype(jnp.float32)
        return 0

    lax.fori_loop(0, last, refill, 0)
    own_copy(last).wait_recv()
    arrived = own_recv[last].astype(jnp.float32)
    mask_sibling = arrived[CHUNK - 8 :, :]
    base[pl.ds(FRONT + last * CHUNK, CHUNK), :] = jnp.where(row >= CHUNK - MARK, 0.0, arrived)
    spread(1)

    def load(place, c, before):
        block = part_recv[place, c].astype(jnp.float32)
        if before is None:
            edge = jnp.zeros((keep, LANES), jnp.float32)
        else:
            edge = part_recv[place, before, :, CHUNK - LANES :].astype(jnp.float32)
        joined = jnp.concatenate([edge, block], axis=1)
        for a in range(GROUPS):
            start = LANES - (GROUPS - 1 - a) * STEP
            lhs[place, a * keep : (a + 1) * keep, :] = joined[:, start : start + CHUNK].astype(
                jnp.bfloat16
            )

    def product(place, c, lanes):
        at = pl.multiple_of(c * CHUNK, CHUNK)
        return jnp.dot(
            lhs[place], shifted[place, pl.ds(at, CHUNK), lanes], preferred_element_type=jnp.float32
        )

    quarters = [slice(q * 2 * rows, (q + 1) * 2 * rows) for q in range(STEP // 2)]

    def arrive(c, before):
        for place, copy in enumerate(part_copies(c)):
            copy.wait_recv()
            load(place, c, before)

    arrive(0, None)
    for lanes in quarters:
        total[:, lanes] = product(0, 0, lanes) + product(1, 0, lanes)

    def middle(c, _):
        arrive(c, c - 1)
        for lanes in quarters:
            total[:, lanes] += product(0, c, lanes) + product(1, c, lanes)
        return 0

    lax.fori_loop(1, last, middle, 0)

    arrive(last, last - 1)
    marks = [
        part_recv[place, last, 0:MARK, CHUNK - LANES :].astype(jnp.float32)[
            0:8, LANES - 1 : LANES
        ]
        for place in range(2)
    ]
    valid = marks[0] * mask + marks[1] * mask_sibling
    scale = (1.0 / (jnp.maximum(valid, 1.0) * math.sqrt(seg_len)))[0:1, :]
    for q, lanes in enumerate(quarters):
        done = total[:, lanes] + product(0, last, lanes) + product(1, last, lanes)
        for s in range(2):
            for a in range(GROUPS):
                out_ref[:, a * STEP + 2 * q + s, :] = (
                    done[a * keep : (a + 1) * keep, s * rows : (s + 1) * rows] * scale
                )

    def drain(c, _):
        for copy in part_copies(c):
            copy.wait_send()
        own_copy(c).wait_send()
        return 0

    lax.fori_loop(0, chunks, drain, 0)


def correlate(bit, rec, assign, mask):
    seg_len, rows = rec.shape
    span = seg_len + LAGS
    span += -span % CHUNK
    chunks = span // CHUNK
    keep = rows // 2
    vmem = pl.BlockSpec(memory_space=pltpu.VMEM)
    return pl.pallas_call(
        functools.partial(kernel, bit),
        out_shape=jax.ShapeDtypeStruct((keep, LAGS, rows), jnp.float32),
        in_specs=[pl.BlockSpec(memory_space=pl.ANY)] * 3,
        out_specs=vmem,
        scratch_shapes=[
            pltpu.VMEM(rec.shape, rec.dtype),
            pltpu.VMEM(assign.shape, assign.dtype),
            pltpu.VMEM(mask.shape, mask.dtype),
            pltpu.VMEM((span + FRONT, rows), jnp.float32),
            pltpu.VMEM((2, span, STEP * rows), jnp.bfloat16),
            pltpu.VMEM((chunks, rows, CHUNK), jnp.bfloat16),
            pltpu.VMEM((2, chunks, keep, CHUNK), jnp.bfloat16),
            pltpu.VMEM((chunks, CHUNK, rows), jnp.bfloat16),
            pltpu.VMEM((chunks, CHUNK, rows), jnp.bfloat16),
            pltpu.VMEM((2, GROUPS * keep, CHUNK), jnp.bfloat16),
            pltpu.VMEM((GROUPS * keep, STEP * rows), jnp.float32),
            pltpu.SemaphoreType.DMA((2, chunks)),
            pltpu.SemaphoreType.DMA((2, chunks)),
            pltpu.SemaphoreType.DMA((chunks,)),
            pltpu.SemaphoreType.DMA((chunks,)),
            pltpu.SemaphoreType.DMA((3,)),
        ],
        compiler_params=pltpu.CompilerParams(
            collective_id=bit, has_side_effects=True, vmem_limit_bytes=48 * 1024 * 1024
        ),
    )(rec, assign, mask)


def body(records, assign, plan, seg_mask):
    rows, segs, seg_len = records.shape
    assert segs == 1 and lax.axis_size("win") == 2
    rec = records.reshape(rows, seg_len).T
    digits = lax.axis_size("chan").bit_length() - 1
    branches = [functools.partial(correlate, bit) for bit in range(digits)]
    normed = lax.switch(plan[0], branches, rec, assign.reshape(1, rows), seg_mask.reshape(1, 1))
    return jnp.transpose(normed, (2, 0, 1))[None]


def solution(mesh):
    placed = (P(("days", "chan"), "win", None), P("chan"), P(), P(("days", "chan"), "win"))
    return jax.shard_map(
        body, mesh=mesh, in_specs=placed, out_specs=P("days", "chan", "win", None), check_vma=False
    )
```
